128 devices in a mesh: freq: 8 (over x, core), rows: 16 (over y, z).
Axes of the slice: x: 4, y: 4, z: 4, core: 2. Of those that a mesh axis runs over, the one named last changes fastest.
Arguments:
- time_loads: float32 [256, 192, 4096], P('freq', None, 'rows'), may hold values from -6 to 6
- factor: float32 [16, 2, 4096, 4096], P('freq', None, 'rows'), may hold values from -0.0625 to 0.0625
- diag_inverse: float32 [16, 2, 4096, 256], P('freq', None, 'rows'), may hold values from -0.25 to 0.25
- pivot_order: int32 [16], replicated, may hold values from 0 to 15, each once
Outputs:
- solution: float32 [16, 2, 192, 4096], P('freq', None, None, 'rows')
The draws below stay inside these ranges and needn't reach their ends.
Inputs may be any that keep to these rules, and one draw needn't show every extreme that they name: `pivot_order`: a permutation of the 16 row blocks.
All inputs are finite; a program needn't handle non-finite values.
Results may differ from the reference program's by a relative error of at most 0.0001.
Values sent between devices are 32-bit elements; how exact they have to be, the bound alone decides.
No kernel may reach another device: no remote copies, remote signals or barrier semaphores. Data moves between devices by JAX's collectives and lax.ppermute only.
A program may use at most 128 MiB of HBM per device.

```python
import jax
import jax.numpy as jnp
from jax import lax

BS = 256
FREQS = 16
STEPS = 256
CASES = 192
NB = 16
ROWS = 4096


def block_scale(stream_key, dims, shards, low, high):
    def one(position, shards_of):
        draws = jax.random.uniform(jax.random.fold_in(jax.random.fold_in(stream_key, 6), position), (shards_of,), jnp.float32, low / len(shards), high / len(shards))
        return jnp.repeat(jnp.exp(draws), dims[position] // shards_of).reshape((-1,) + (1,) * (len(dims) - position - 1))

    level = one(*shards[0])
    for cut in shards[1:]:
        level = level * one(*cut)
    return level


def gaussian(rng, extent, scale, reach, shards=(), held_as=jnp.bfloat16):
    gain = block_scale(rng, extent, shards, -0.22, 0.18) if shards else 1.0
    array = jax.random.normal(rng, extent, jnp.float32) * scale * gain
    return jnp.minimum(jnp.maximum(array, -reach), reach).astype(held_as)


def setup_inputs(seed: int = 0) -> dict:
    splits = jax.random.split(jax.random.key(seed), 5)
    return {
        "time_loads": gaussian(splits[0], (STEPS, CASES, ROWS), 1.0, 6.0, ((0, 8), (2, 16)), jnp.float32),
        "factor": gaussian(splits[1], (FREQS, 2, ROWS, ROWS), (2 * ROWS) ** -0.5, 0.0625, ((0, 8), (2, 16)), jnp.float32),
        "diag_inverse": gaussian(splits[2], (FREQS, 2, ROWS, BS), (2 * BS) ** -0.5, 0.25, ((0, 8), (2, 16)), jnp.float32),
        "pivot_order": jax.random.permutation(splits[3], NB).astype(jnp.int32),
    }


def tables(count, length):
    freq_range = jnp.arange(count, dtype=jnp.float32)
    step_range = jnp.arange(length, dtype=jnp.float32)
    angles = 2.0 * jnp.pi * ((freq_range[:, None] * step_range[None, :]) % length) / length
    damping = jnp.exp(step_range * (jnp.log(0.1) / length))
    return jnp.cos(angles) * damping[None, :], -jnp.sin(angles) * damping[None, :]


def product(matrix, vector):
    return jnp.einsum("fab,fcb->fca", matrix, vector, precision=lax.Precision.HIGHEST)


def complex_apply(matrix, vector):
    matrix_real, matrix_imag = matrix[:, 0], matrix[:, 1]
    vector_real, vector_imag = vector[:, 0], vector[:, 1]
    real_part = product(matrix_real, vector_real) - product(matrix_imag, vector_imag)
    imag_part = product(matrix_real, vector_imag) + product(matrix_imag, vector_real)
    return jnp.stack([real_part, imag_part], axis=1)


def reference(time_loads, factor, diag_inverse, pivot_order):
    cosine_table, sine_table = tables(FREQS, STEPS)
    spectra = jnp.stack([
        jnp.einsum("fn,ncr->fcr", cosine_table, time_loads, precision=lax.Precision.HIGHEST),
        jnp.einsum("fn,ncr->fcr", sine_table, time_loads, precision=lax.Precision.HIGHEST)], axis=1)
    residual = spectra
    solution = jnp.zeros_like(spectra)
    for turn in range(NB):
        first_row = (pivot_order[turn] * BS).astype(jnp.int32)
        current = lax.dynamic_slice_in_dim(residual, first_row, BS, 3)
        inverse_block = lax.dynamic_slice_in_dim(diag_inverse, first_row, BS, 2)
        solved = complex_apply(inverse_block, current)
        solution = lax.dynamic_update_slice_in_dim(solution, solved, first_row, 3)
        column = lax.dynamic_slice_in_dim(factor, first_row, BS, 3)
        residual = residual - complex_apply(column, solved)
    return solution
```

```python
import jax
import jax.numpy as jnp
from jax import lax
from jax.sharding import PartitionSpec as P

FREQS = 16
STEPS = 256
BS = 256
NB = 16
CASES = 192
GROUPS = 8
GC = CASES // GROUPS
SPAN = 2
HIGH = lax.Precision.HIGH


def tables(count, length):
    freq_range = jnp.arange(count, dtype=jnp.float32)
    step_range = jnp.arange(length, dtype=jnp.float32)
    angles = 2.0 * jnp.pi * (freq_range[:, None] * step_range[None, :] % length) / length
    damping = jnp.exp(step_range * (jnp.log(0.1) / length))
    return (jnp.cos(angles) * damping[None, :], -jnp.sin(angles) * damping[None, :])


def ring(value, step):
    return lax.ppermute(value, "freq", [(i, (i + 2 * step) % 8) for i in range(8)])


def swap(value):
    return lax.ppermute(value, "freq", [(i, i ^ 1) for i in range(8)])


def spectra_of(time_loads):
    me = lax.axis_index("freq")
    chip, core = me // 2, me % 2
    half = CASES // 2
    mine = lax.dynamic_slice_in_dim(time_loads, core * half, half, 1)
    other = swap(lax.dynamic_slice_in_dim(time_loads, (1 - core) * half, half, 1))
    cosine, sine = tables(FREQS, STEPS)
    table = jnp.stack([cosine, sine], axis=0)
    here = lax.dynamic_slice_in_dim(table, me * 32, 32, 2)
    there = lax.dynamic_slice_in_dim(table, (me ^ 1) * 32, 32, 2)
    weights = jnp.concatenate([here, there], axis=2)
    loads = jnp.concatenate([mine, other], axis=0).reshape(64, GROUPS // 2, GC, BS)
    part = jnp.einsum("pfn,ngck->fgpck", weights, loads, precision=HIGH)
    part = part.reshape(4, 4, GROUPS // 2, 2, GC, BS)

    def to(offset):
        return lax.dynamic_index_in_dim(part, (chip + offset) % 4, 0, False)

    far = to(2)
    from_left = ring(far[:2], 1)
    from_right = ring(far[2:], -1)
    right, left = to(1), to(3)
    right = jnp.concatenate([right[:2] + from_left, right[2:]], axis=0)
    left = jnp.concatenate([left[:2], left[2:] + from_right], axis=0)
    total = to(0) + ring(right, 1) + ring(left, -1)
    total = total.reshape(2, 2, GROUPS // 2, 2, GC, BS)
    keep = lax.dynamic_index_in_dim(total, core, 0, False)
    got = swap(lax.dynamic_index_in_dim(total, 1 - core, 0, False))
    pair = jnp.where(core == 0, jnp.stack([keep, got], 1), jnp.stack([got, keep], 1))
    return pair.reshape(2, GROUPS, 2, GC, BS)


def apply(matrix, vector):
    out = jnp.einsum("fpab,fgqcb->fgqcpa", matrix, vector, precision=HIGH)
    real = out[:, :, 0, :, 0] - out[:, :, 1, :, 1]
    imag = out[:, :, 1, :, 0] + out[:, :, 0, :, 1]
    return jnp.stack([real, imag], axis=2)


def body(time_loads, factor, diag_inverse, pivot_order):
    my_block = lax.axis_index("rows")
    my_freq = my_block // GROUPS
    my_place = jnp.sum(jnp.where(pivot_order == my_block, jnp.arange(NB, dtype=jnp.int32), 0))
    before = pivot_order[jnp.maximum(my_place - 1, 0)]
    below = lax.dynamic_slice_in_dim(factor, before * BS, BS, 3)
    prod = jnp.einsum("fpab,fqbc->fpqac", diag_inverse, below, precision=HIGH)
    coupling = jnp.stack([prod[:, 0, 0] - prod[:, 1, 1], prod[:, 0, 1] + prod[:, 1, 0]], axis=1)
    couplings = lax.all_gather(coupling, "rows", axis=0)

    residual = spectra_of(time_loads)
    columns = [lax.dynamic_slice_in_dim(factor, pivot_order[k] * BS, BS, 3) for k in range(NB)]

    solved = []
    for first in range(0, NB, SPAN):
        scaled = apply(diag_inverse, residual).reshape(NB, 2, GC, BS)
        spread = lax.all_to_all(scaled, "rows", 0, 0, tiled=True)
        x0 = lax.dynamic_index_in_dim(spread, pivot_order[first], 0, False)
        x1 = lax.dynamic_index_in_dim(spread, pivot_order[first + 1], 0, False)
        link = couplings[pivot_order[first + 1], my_freq]
        x1 = x1 - apply(link[None], x0[None, None])[0, 0]
        block = jnp.concatenate([x0, x1], axis=2)
        block = jnp.broadcast_to(block[None], (NB,) + block.shape)
        block = lax.all_to_all(block, "rows", 0, 0, tiled=True)
        solved.append(block)
        if first + SPAN < NB:
            column = jnp.concatenate(columns[first : first + SPAN], axis=3)
            residual = residual - apply(column, block.reshape(2, GROUPS, 2, GC, SPAN * BS))

    def pick(place):
        at = place % SPAN
        return lambda blocks: blocks[place // SPAN][..., at * BS : (at + 1) * BS]

    own = lax.switch(my_place, [pick(i) for i in range(NB)], solved)
    own = own.reshape(2, GROUPS, 2, GC, BS).transpose(0, 2, 1, 3, 4)
    return own.reshape(2, 2, CASES, BS)


def solution(mesh):
    placed = (
        P("freq", None, "rows"),
        P("freq", None, "rows", None),
        P("freq", None, "rows", None),
        P(),
    )
    return jax.shard_map(
        body, mesh=mesh, in_specs=placed, out_specs=P("freq", None, None, "rows"), check_vma=False
    )
```

```python
import functools

import jax
import jax.numpy as jnp
from jax import lax
from jax.experimental import pallas as pl
from jax.experimental.pallas import tpu as pltpu
from jax.sharding import PartitionSpec as P

FREQS = 16
STEPS = 256
BS = 256
NB = 16
CASES = 192
GROUPS = 8
GC = CASES // GROUPS
SPAN = 2
PAIRS = (NB - 1) // SPAN
WIDE = 50 << 20
NARROW = 12 << 20
HIGH = lax.Precision.HIGH


def tables(count, length):
    freq_range = jnp.arange(count, dtype=jnp.float32)
    step_range = jnp.arange(length, dtype=jnp.float32)
    angles = 2.0 * jnp.pi * (freq_range[:, None] * step_range[None, :] % length) / length
    damping = jnp.exp(step_range * (jnp.log(0.1) / length))
    return (jnp.cos(angles) * damping[None, :], -jnp.sin(angles) * damping[None, :])


def ring(value, step):
    return lax.ppermute(value, "freq", [(i, (i + 2 * step) % 8) for i in range(8)])


def swap(value):
    return lax.ppermute(value, "freq", [(i, i ^ 1) for i in range(8)])


def partial_spectra(time_loads, other):
    me = lax.axis_index("freq")
    core = me % 2
    half = CASES // 2
    mine = jnp.where(core == 0, time_loads[:, :half], time_loads[:, half:])
    cosine, sine = tables(FREQS, STEPS)
    table = jnp.stack([cosine, sine], axis=0)
    here = lax.dynamic_slice_in_dim(table, me * 32, 32, 2)
    there = lax.dynamic_slice_in_dim(table, (me ^ 1) * 32, 32, 2)
    weights = jnp.concatenate([here, there], axis=2)
    loads = jnp.concatenate([mine, other], axis=0).reshape(64, GROUPS // 2, GC, BS)
    part = jnp.einsum("pfn,ngck->fgpck", weights, loads, precision=HIGH)
    return part.reshape(4, 4, GROUPS // 2, 2, GC, BS)


def reduced(part, order, factor):
    me = lax.axis_index("freq")
    chip, core = me // 2, me % 2

    def to(offset):
        return lax.dynamic_index_in_dim(part, (chip + offset) % 4, 0, False)

    far = to(2)
    from_left = ring(far[:2], 1)
    from_right = ring(far[2:], -1)
    right, left = to(1), to(3)
    right = jnp.concatenate([right[:2] + from_left, right[2:]], axis=0)
    left = jnp.concatenate([left[:2], left[2:] + from_right], axis=0)
    right, left, order = lax.optimization_barrier((right, left, order))
    ordered = reorder(order, factor)
    right, left, ordered = lax.optimization_barrier((ring(right, 1), ring(left, -1), ordered))
    total = to(0) + right + left
    total = total.reshape(2, 2, GROUPS // 2, 2, GC, BS)
    keep = lax.dynamic_index_in_dim(total, core, 0, False)
    got = swap(lax.dynamic_index_in_dim(total, 1 - core, 0, False))
    pair = jnp.where(core == 0, jnp.stack([keep, got], 1), jnp.stack([got, keep], 1))
    return pair.reshape(NB, 2, GC, BS), ordered


def split(value):
    high = value.astype(jnp.bfloat16)
    return high, (value - high.astype(jnp.float32)).astype(jnp.bfloat16)


def dot3(left, right, contract):
    dims = (((1,), (contract,)), ((), ()))

    def one(a, b):
        return lax.dot_general(a, b, dims, preferred_element_type=jnp.float32)

    return one(left[0], right[0]) + (one(left[0], right[1]) + one(left[1], right[0]))


def coupling_kernel(order_ref, inverse_ref, factor_ref, out_ref, below_ref, sem):
    me = lax.axis_index("rows")
    before = order_ref[0]
    for k in range(1, NB):
        before = jnp.where(order_ref[k] == me, order_ref[k - 1], before)
    at = pl.ds(pl.multiple_of(before * BS, BS), BS)
    copy = pltpu.make_async_copy(factor_ref.at[:, :, :, at], below_ref, sem)
    copy.start()
    copy.wait()
    for f in range(2):
        d_real, d_imag = split(inverse_ref[f, 0]), split(inverse_ref[f, 1])
        b_real, b_imag = split(below_ref[f, 0]), split(below_ref[f, 1])
        out_ref[f, 0] = dot3(d_real, b_real, 0) - dot3(d_imag, b_imag, 0)
        out_ref[f, 1] = dot3(d_real, b_imag, 0) + dot3(d_imag, b_real, 0)


def coupling_of(order, diag_inverse, factor):
    return pl.pallas_call(
        coupling_kernel,
        in_specs=[
            pl.BlockSpec(memory_space=pltpu.SMEM),
            pl.BlockSpec(memory_space=pltpu.VMEM),
            pl.BlockSpec(memory_space=pl.ANY),
        ],
        out_specs=pl.BlockSpec(memory_space=pltpu.VMEM),
        out_shape=jax.ShapeDtypeStruct((2, 2, BS, BS), jnp.float32),
        scratch_shapes=[pltpu.VMEM((2, 2, BS, BS), jnp.float32), pltpu.SemaphoreType.DMA],
        compiler_params=pltpu.CompilerParams(vmem_limit_bytes=WIDE),
        cost_estimate=pl.CostEstimate(flops=48 * BS**3, bytes_accessed=3 << 20, transcendentals=0),
        name="coupling",
    )(order, diag_inverse, factor)


def reorder_kernel(order_ref, factor_ref, *refs):
    outs, (held, in_sems, out_sems) = refs[: PAIRS + 1], refs[PAIRS + 1 :]
    reads, writes = [], []
    for k in range(NB - 1):
        at = pl.ds(pl.multiple_of(order_ref[k] * BS, BS), BS)
        reads.append(pltpu.make_async_copy(factor_ref.at[:, :, :, at], held.at[k], in_sems.at[k]))
        reads[k].start()
        side = (k + 1) % SPAN * BS if k else 0
        out = outs[(k + 1) // SPAN].at[:, :, :, side : side + BS]
        writes.append(pltpu.make_async_copy(held.at[k], out, out_sems.at[k]))
    for read, write in zip(reads, writes):
        read.wait()
        write.start()
    for write in writes:
        write.wait()


def reorder(order, factor):
    shapes = [jax.ShapeDtypeStruct((2, 2, BS, (SPAN if i else 1) * BS), jnp.float32) for i in range(PAIRS + 1)]
    return pl.pallas_call(
        reorder_kernel,
        in_specs=[pl.BlockSpec(memory_space=pltpu.SMEM), pl.BlockSpec(memory_space=pl.ANY)],
        out_specs=[pl.BlockSpec(memory_space=pl.ANY)] * (PAIRS + 1),
        out_shape=shapes,
        scratch_shapes=[
            pltpu.VMEM((NB - 1, 2, 2, BS, BS), jnp.float32),
            pltpu.SemaphoreType.DMA((NB - 1,)),
            pltpu.SemaphoreType.DMA((NB - 1,)),
        ],
        compiler_params=pltpu.CompilerParams(vmem_limit_bytes=WIDE),
        cost_estimate=pl.CostEstimate(flops=0, bytes_accessed=32 << 20, transcendentals=0),
        name="reorder",
    )(order, factor)


def links_kernel(order_ref, gathered_ref, *refs):
    outs, sems = refs[:PAIRS], refs[PAIRS]
    freq = lax.axis_index("rows") // GROUPS
    copies = []
    for pair in range(PAIRS):
        copies.append(
            pltpu.make_async_copy(gathered_ref.at[order_ref[SPAN * (pair + 1)], freq], outs[pair], sems.at[pair])
        )
        copies[-1].start()
    for copy in copies:
        copy.wait()


def links_of(order, gathered):
    return pl.pallas_call(
        links_kernel,
        in_specs=[pl.BlockSpec(memory_space=pltpu.SMEM), pl.BlockSpec(memory_space=pl.ANY)],
        out_specs=[pl.BlockSpec(memory_space=pl.ANY)] * PAIRS,
        out_shape=[jax.ShapeDtypeStruct((2, BS, BS), jnp.float32)] * PAIRS,
        scratch_shapes=[pltpu.SemaphoreType.DMA((PAIRS,))],
        compiler_params=pltpu.CompilerParams(vmem_limit_bytes=WIDE),
        cost_estimate=pl.CostEstimate(flops=0, bytes_accessed=8 << 20, transcendentals=0),
        name="links",
    )(order, gathered)


def local(kernel, shape, flops, name, *operands, scalars=0):
    specs = [pl.BlockSpec(memory_space=pltpu.SMEM)] * scalars
    specs += [pl.BlockSpec(memory_space=pltpu.VMEM)] * (len(operands) - scalars)
    return pl.pallas_call(
        kernel,
        in_specs=specs,
        out_specs=pl.BlockSpec(memory_space=pltpu.VMEM),
        out_shape=jax.ShapeDtypeStruct(shape, jnp.float32),
        compiler_params=pltpu.CompilerParams(vmem_limit_bytes=NARROW),
        cost_estimate=pl.CostEstimate(flops=flops, bytes_accessed=1 << 20, transcendentals=0),
        name=name,
    )(*operands)


def apply(matrix, vector):
    out = jnp.einsum("fpab,fgqcb->fgqcpa", matrix, vector, precision=HIGH)
    real = out[:, :, 0, :, 0] - out[:, :, 1, :, 1]
    imag = out[:, :, 1, :, 0] + out[:, :, 0, :, 1]
    return jnp.stack([real, imag], axis=2)


def solve_kernel(pair, order_ref, spread_ref, link_ref, out_ref):
    first = spread_ref[order_ref[SPAN * pair + 1]]
    second = spread_ref[order_ref[SPAN * pair + 2]]
    rows = split(first.reshape(2 * GC, BS))
    by_real, by_imag = [dot3(rows, split(link_ref[p]), 1).reshape(2, GC, BS) for p in range(2)]
    real = second[0] - (by_real[0] - by_imag[1])
    imag = second[1] - (by_real[1] + by_imag[0])
    out_ref[:, :, :BS] = first
    out_ref[0, :, BS:] = real
    out_ref[1, :, BS:] = imag


def solve(order, spread, link, pair):
    kernel = functools.partial(solve_kernel, pair)
    shape = (2, GC, SPAN * BS)
    return local(kernel, shape, 24 * BS * BS * GC, "solve", order, spread, link, scalars=1)


def exchange(value):
    return lax.all_to_all(value, "rows", 0, 0, tiled=True)


def body(time_loads, factor, diag_inverse, pivot_order):
    my_block = lax.axis_index("rows")
    my_place = jnp.sum(jnp.where(pivot_order == my_block, jnp.arange(NB, dtype=jnp.int32), 0))
    half = CASES // 2
    core = lax.axis_index("freq") % 2
    coupling = coupling_of(pivot_order, diag_inverse, factor)
    gathered = lax.all_gather(coupling, "rows", axis=0)
    other = swap(jnp.where(core == 0, time_loads[:, half:], time_loads[:, :half]))
    part = partial_spectra(time_loads, other)
    residual, ordered = reduced(part, pivot_order, factor)
    residual = residual.reshape(2, GROUPS, 2, GC, BS)

    def spread():
        return exchange(apply(diag_inverse, residual).reshape(NB, 2, GC, BS))

    def updated(columns, block):
        return residual - apply(columns, block.reshape(2, GROUPS, 2, GC, -1))

    def share(block):
        return exchange(jnp.broadcast_to(block[None], (NB,) + block.shape))

    solved = [share(lax.dynamic_index_in_dim(spread(), pivot_order[0], 0, False))]
    residual = updated(ordered[0], solved[0])
    links = links_of(pivot_order, gathered)
    for pair in range(PAIRS):
        block = share(solve(pivot_order, spread(), links[pair], pair))
        solved.append(block)
        residual = updated(ordered[pair + 1], block)
    scaled = apply(diag_inverse, residual).reshape(NB, 2, GC, BS)

    def pick(place):
        at = (place + 1) % SPAN
        return lambda scaled, blocks: blocks[(place + 1) // SPAN][..., at * BS * (place > 0) :][..., :BS]

    own = lax.switch(my_place, [pick(i) for i in range(NB - 1)] + [lambda scaled, blocks: scaled], scaled, solved)
    own = own.reshape(2, GROUPS, 2, GC, BS).transpose(0, 2, 1, 3, 4)
    return own.reshape(2, 2, CASES, BS)


def solution(mesh):
    placed = (
        P("freq", None, "rows"),
        P("freq", None, "rows", None),
        P("freq", None, "rows", None),
        P(),
    )
    return jax.shard_map(
        body, mesh=mesh, in_specs=placed, out_specs=P("freq", None, None, "rows"), check_vma=False
    )
```

```python
import functools

import jax
import jax.numpy as jnp
from jax import lax
from jax.experimental import pallas as pl
from jax.experimental.pallas import tpu as pltpu
from jax.sharding import PartitionSpec as P

FREQS = 16
STEPS = 256
BS = 256
NB = 16
CASES = 192
GROUPS = 8
GC = CASES // GROUPS
SPAN = 2
PAIRS = (NB - 1) // SPAN
HALF = CASES // 2
CUTS = 4
WIDE = 50 << 20
NARROW = 12 << 20
HIGH = lax.Precision.HIGH


def tables(count, length):
    freq_range = jnp.arange(count, dtype=jnp.float32)
    step_range = jnp.arange(length, dtype=jnp.float32)
    angles = 2.0 * jnp.pi * (freq_range[:, None] * step_range[None, :] % length) / length
    damping = jnp.exp(step_range * (jnp.log(0.1) / length))
    return (jnp.cos(angles) * damping[None, :], -jnp.sin(angles) * damping[None, :])


def ring(value, step):
    return lax.ppermute(value, "freq", [(i, (i + 2 * step) % 8) for i in range(8)])


def swap(value):
    return lax.ppermute(value, "freq", [(i, i ^ 1) for i in range(8)])


def half_kernel(other, loads_ref, out_ref, held, in_sems, out_sems):
    core = lax.axis_index("freq") % 2
    side = 1 - core if other else core
    at = pl.ds(pl.multiple_of(side * HALF, HALF), HALF)
    reads, writes = [], []
    for i in range(CUTS):
        steps = slice(i * 32 // CUTS, (i + 1) * 32 // CUTS)
        reads.append(pltpu.make_async_copy(loads_ref.at[steps, at], held.at[i], in_sems.at[i]))
        reads[i].start()
        writes.append(pltpu.make_async_copy(held.at[i], out_ref.at[steps], out_sems.at[i]))
    for read, write in zip(reads, writes):
        read.wait()
        write.start()
    for write in writes:
        write.wait()


def half_of(loads, other):
    return pl.pallas_call(
        functools.partial(half_kernel, other),
        in_specs=[pl.BlockSpec(memory_space=pl.ANY)],
        out_specs=pl.BlockSpec(memory_space=pl.ANY),
        out_shape=jax.ShapeDtypeStruct((32, HALF, BS), jnp.float32),
        scratch_shapes=[
            pltpu.VMEM((CUTS, 32 // CUTS, HALF, BS), jnp.float32),
            pltpu.SemaphoreType.DMA((CUTS,)),
            pltpu.SemaphoreType.DMA((CUTS,)),
        ],
        compiler_params=pltpu.CompilerParams(vmem_limit_bytes=57 << 20),
        cost_estimate=pl.CostEstimate(flops=0, bytes_accessed=6 << 20, transcendentals=0),
        name="half",
    )(loads)


def partial_spectra(mine, other):
    me = lax.axis_index("freq")
    cosine, sine = tables(FREQS, STEPS)
    table = jnp.stack([cosine, sine], axis=1)
    here = lax.dynamic_slice_in_dim(table, me * 32, 32, 2)
    there = lax.dynamic_slice_in_dim(table, (me ^ 1) * 32, 32, 2)
    weights = jnp.concatenate([here, there], axis=2).reshape(4, 4, 2, 64)
    loads = jnp.concatenate([mine, other], axis=0)
    return jnp.einsum("dfpn,nck->cdfpk", weights, loads, precision=HIGH)


def reduced(part, order, factor):
    me = lax.axis_index("freq")
    chip, core = me // 2, me % 2
    cut = HALF // 2

    def to(offset):
        return lax.dynamic_index_in_dim(part, (chip + offset) % 4, 1, False)

    far = to(2)
    from_left = ring(far[:cut], 1)
    from_right = ring(far[cut:], -1)
    right, left = to(1), to(3)
    right = jnp.concatenate([right[:cut] + from_left, right[cut:]], axis=0)
    left = jnp.concatenate([left[:cut], left[cut:] + from_right], axis=0)
    right, left, order = lax.optimization_barrier((right, left, order))
    ordered = reorder(order, factor)
    right, left, ordered = lax.optimization_barrier((ring(right, 1), ring(left, -1), ordered))
    total = to(0) + right + left
    total = total.reshape(GROUPS // 2, GC, 2, 2, 2, BS).transpose(2, 3, 0, 4, 1, 5)
    keep = lax.dynamic_index_in_dim(total, core, 0, False)
    got = swap(lax.dynamic_index_in_dim(total, 1 - core, 0, False))
    pair = jnp.where(core == 0, jnp.stack([keep, got], 1), jnp.stack([got, keep], 1))
    return pair.reshape(NB, 2, GC, BS), ordered


def split(value):
    high = value.astype(jnp.bfloat16)
    return high, (value - high.astype(jnp.float32)).astype(jnp.bfloat16)


def dot3(left, right, contract):
    dims = (((1,), (contract,)), ((), ()))

    def one(a, b):
        return lax.dot_general(a, b, dims, preferred_element_type=jnp.float32)

    return one(left[0], right[0]) + (one(left[0], right[1]) + one(left[1], right[0]))


def coupling_kernel(order_ref, inverse_ref, factor_ref, out_ref, below_ref, sem):
    me = lax.axis_index("rows")
    before = order_ref[0]
    for k in range(1, NB):
        before = jnp.where(order_ref[k] == me, order_ref[k - 1], before)
    at = pl.ds(pl.multiple_of(before * BS, BS), BS)
    copy = pltpu.make_async_copy(factor_ref.at[:, :, :, at], below_ref, sem)
    copy.start()
    copy.wait()
    for f in range(2):
        d_real, d_imag = split(inverse_ref[f, 0]), split(inverse_ref[f, 1])
        b_real, b_imag = split(below_ref[f, 0]), split(below_ref[f, 1])
        out_ref[f, 0] = dot3(d_real, b_real, 0) - dot3(d_imag, b_imag, 0)
        out_ref[f, 1] = dot3(d_real, b_imag, 0) + dot3(d_imag, b_real, 0)


def coupling_of(order, diag_inverse, factor):
    return pl.pallas_call(
        coupling_kernel,
        in_specs=[
            pl.BlockSpec(memory_space=pltpu.SMEM),
            pl.BlockSpec(memory_space=pltpu.VMEM),
            pl.BlockSpec(memory_space=pl.ANY),
        ],
        out_specs=pl.BlockSpec(memory_space=pltpu.VMEM),
        out_shape=jax.ShapeDtypeStruct((2, 2, BS, BS), jnp.float32),
        scratch_shapes=[pltpu.VMEM((2, 2, BS, BS), jnp.float32), pltpu.SemaphoreType.DMA],
        compiler_params=pltpu.CompilerParams(vmem_limit_bytes=WIDE),
        cost_estimate=pl.CostEstimate(flops=48 * BS**3, bytes_accessed=3 << 20, transcendentals=0),
        name="coupling",
    )(order, diag_inverse, factor)


def reorder_kernel(order_ref, factor_ref, *refs):
    outs, (held, in_sems, out_sems) = refs[: PAIRS + 1], refs[PAIRS + 1 :]
    reads, writes = [], []
    for k in range(NB - 1):
        at = pl.ds(pl.multiple_of(order_ref[k] * BS, BS), BS)
        reads.append(pltpu.make_async_copy(factor_ref.at[:, :, :, at], held.at[k], in_sems.at[k]))
        reads[k].start()
        side = (k + 1) % SPAN * BS if k else 0
        out = outs[(k + 1) // SPAN].at[:, :, :, side : side + BS]
        writes.append(pltpu.make_async_copy(held.at[k], out, out_sems.at[k]))
    for read, write in zip(reads, writes):
        read.wait()
        write.start()
    for write in writes:
        write.wait()


def reorder(order, factor):
    shapes = [jax.ShapeDtypeStruct((2, 2, BS, (SPAN if i else 1) * BS), jnp.float32) for i in range(PAIRS + 1)]
    return pl.pallas_call(
        reorder_kernel,
        in_specs=[pl.BlockSpec(memory_space=pltpu.SMEM), pl.BlockSpec(memory_space=pl.ANY)],
        out_specs=[pl.BlockSpec(memory_space=pl.ANY)] * (PAIRS + 1),
        out_shape=shapes,
        scratch_shapes=[
            pltpu.VMEM((NB - 1, 2, 2, BS, BS), jnp.float32),
            pltpu.SemaphoreType.DMA((NB - 1,)),
            pltpu.SemaphoreType.DMA((NB - 1,)),
        ],
        compiler_params=pltpu.CompilerParams(vmem_limit_bytes=WIDE),
        cost_estimate=pl.CostEstimate(flops=0, bytes_accessed=32 << 20, transcendentals=0),
        name="reorder",
    )(order, factor)


def links_kernel(order_ref, gathered_ref, *refs):
    outs, sems = refs[:PAIRS], refs[PAIRS]
    freq = lax.axis_index("rows") // GROUPS
    copies = []
    for pair in range(PAIRS):
        copies.append(
            pltpu.make_async_copy(gathered_ref.at[order_ref[SPAN * (pair + 1)], freq], outs[pair], sems.at[pair])
        )
        copies[-1].start()
    for copy in copies:
        copy.wait()


def links_of(order, gathered):
    return pl.pallas_call(
        links_kernel,
        in_specs=[pl.BlockSpec(memory_space=pltpu.SMEM), pl.BlockSpec(memory_space=pl.ANY)],
        out_specs=[pl.BlockSpec(memory_space=pl.ANY)] * PAIRS,
        out_shape=[jax.ShapeDtypeStruct((2, BS, BS), jnp.float32)] * PAIRS,
        scratch_shapes=[pltpu.SemaphoreType.DMA((PAIRS,))],
        compiler_params=pltpu.CompilerParams(vmem_limit_bytes=WIDE),
        cost_estimate=pl.CostEstimate(flops=0, bytes_accessed=8 << 20, transcendentals=0),
        name="links",
    )(order, gathered)


def local(kernel, shape, flops, name, *operands, scalars=0):
    specs = [pl.BlockSpec(memory_space=pltpu.SMEM)] * scalars
    specs += [pl.BlockSpec(memory_space=pltpu.VMEM)] * (len(operands) - scalars)
    return pl.pallas_call(
        kernel,
        in_specs=specs,
        out_specs=pl.BlockSpec(memory_space=pltpu.VMEM),
        out_shape=jax.ShapeDtypeStruct(shape, jnp.float32),
        compiler_params=pltpu.CompilerParams(vmem_limit_bytes=NARROW),
        cost_estimate=pl.CostEstimate(flops=flops, bytes_accessed=1 << 20, transcendentals=0),
        name=name,
    )(*operands)


def apply(matrix, vector):
    out = jnp.einsum("fpab,fgqcb->fgqcpa", matrix, vector, precision=HIGH)
    real = out[:, :, 0, :, 0] - out[:, :, 1, :, 1]
    imag = out[:, :, 1, :, 0] + out[:, :, 0, :, 1]
    return jnp.stack([real, imag], axis=2)


def solve_kernel(pair, order_ref, spread_ref, link_ref, out_ref):
    first = spread_ref[order_ref[SPAN * pair + 1]]
    second = spread_ref[order_ref[SPAN * pair + 2]]
    rows = split(first.reshape(2 * GC, BS))
    by_real, by_imag = [dot3(rows, split(link_ref[p]), 1).reshape(2, GC, BS) for p in range(2)]
    real = second[0] - (by_real[0] - by_imag[1])
    imag = second[1] - (by_real[1] + by_imag[0])
    out_ref[:, :, :BS] = first
    out_ref[0, :, BS:] = real
    out_ref[1, :, BS:] = imag


def solve(order, spread, link, pair):
    kernel = functools.partial(solve_kernel, pair)
    shape = (2, GC, SPAN * BS)
    return local(kernel, shape, 24 * BS * BS * GC, "solve", order, spread, link, scalars=1)


def exchange(value):
    return lax.all_to_all(value, "rows", 0, 0, tiled=True)


def body(time_loads, factor, diag_inverse, pivot_order):
    my_block = lax.axis_index("rows")
    my_place = jnp.sum(jnp.where(pivot_order == my_block, jnp.arange(NB, dtype=jnp.int32), 0))
    sent, order, time_loads = lax.optimization_barrier((half_of(time_loads, True), pivot_order, time_loads))
    other = swap(sent)
    coupling = coupling_of(order, diag_inverse, factor)
    gathered = lax.all_gather(coupling, "rows", axis=0)
    part = partial_spectra(half_of(time_loads, False), other)
    residual, ordered = reduced(part, pivot_order, factor)
    residual = residual.reshape(2, GROUPS, 2, GC, BS)

    def spread():
        return exchange(apply(diag_inverse, residual).reshape(NB, 2, GC, BS))

    def updated(columns, block):
        return residual - apply(columns, block.reshape(2, GROUPS, 2, GC, -1))

    def share(block):
        return exchange(jnp.broadcast_to(block[None], (NB,) + block.shape))

    block = share(lax.dynamic_index_in_dim(spread(), pivot_order[0], 0, False))
    residual = updated(ordered[0], block)
    own = block
    links = links_of(pivot_order, gathered)
    for pair in range(PAIRS):
        block = share(solve(pivot_order, spread(), links[pair], pair))
        place = SPAN * pair + 1
        pick = jnp.where(my_place == place, block[..., :BS], block[..., BS:])
        own = jnp.where((my_place == place) | (my_place == place + 1), pick, own)
        residual = updated(ordered[pair + 1], block)
    last = apply(diag_inverse, residual).reshape(NB, 2, GC, BS)
    own = jnp.where(my_place == NB - 1, last, own)
    own = own.reshape(2, GROUPS, 2, GC, BS).transpose(0, 2, 1, 3, 4)
    return own.reshape(2, 2, CASES, BS)


def solution(mesh):
    placed = (
        P("freq", None, "rows"),
        P("freq", None, "rows", None),
        P("freq", None, "rows", None),
        P(),
    )
    return jax.shard_map(
        body, mesh=mesh, in_specs=placed, out_specs=P("freq", None, None, "rows"), check_vma=False
    )
```

```python
import functools

import jax
import jax.numpy as jnp
from jax import lax
from jax.experimental import pallas as pl
from jax.experimental.pallas import tpu as pltpu
from jax.sharding import PartitionSpec as P

FREQS = 16
STEPS = 256
BS = 256
NB = 16
CASES = 192
GROUPS = 8
GC = CASES // GROUPS
SPAN = 2
PAIRS = (NB - 1) // SPAN
HALF = CASES // 2
CUTS = 4
WIDE = 50 << 20
NARROW = 12 << 20
HIGH = lax.Precision.HIGH


def tables(count, length):
    freq_range = jnp.arange(count, dtype=jnp.float32)
    step_range = jnp.arange(length, dtype=jnp.float32)
    angles = 2.0 * jnp.pi * (freq_range[:, None] * step_range[None, :] % length) / length
    damping = jnp.exp(step_range * (jnp.log(0.1) / length))
    return (jnp.cos(angles) * damping[None, :], -jnp.sin(angles) * damping[None, :])


def ring(value, step):
    return lax.ppermute(value, "freq", [(i, (i + 2 * step) % 8) for i in range(8)])


def swap(value):
    return lax.ppermute(value, "freq", [(i, i ^ 1) for i in range(8)])


def half_kernel(other, loads_ref, out_ref, held, in_sems, out_sems):
    core = lax.axis_index("freq") % 2
    side = 1 - core if other else core
    at = pl.ds(pl.multiple_of(side * HALF, HALF), HALF)
    reads, writes = [], []
    for i in range(CUTS):
        steps = slice(i * 32 // CUTS, (i + 1) * 32 // CUTS)
        reads.append(pltpu.make_async_copy(loads_ref.at[steps, at], held.at[i], in_sems.at[i]))
        reads[i].start()
        writes.append(pltpu.make_async_copy(held.at[i], out_ref.at[steps], out_sems.at[i]))
    for read, write in zip(reads, writes):
        read.wait()
        write.start()
    for write in writes:
        write.wait()


def half_of(loads, other):
    return pl.pallas_call(
        functools.partial(half_kernel, other),
        in_specs=[pl.BlockSpec(memory_space=pl.ANY)],
        out_specs=pl.BlockSpec(memory_space=pl.ANY),
        out_shape=jax.ShapeDtypeStruct((32, HALF, BS), jnp.float32),
        scratch_shapes=[
            pltpu.VMEM((CUTS, 32 // CUTS, HALF, BS), jnp.float32),
            pltpu.SemaphoreType.DMA((CUTS,)),
            pltpu.SemaphoreType.DMA((CUTS,)),
        ],
        compiler_params=pltpu.CompilerParams(vmem_limit_bytes=57 << 20),
        cost_estimate=pl.CostEstimate(flops=0, bytes_accessed=6 << 20, transcendentals=0),
        name="half",
    )(loads)


def partial_spectra(mine, other):
    me = lax.axis_index("freq")
    cosine, sine = tables(FREQS, STEPS)
    table = jnp.stack([cosine, sine], axis=1)
    here = lax.dynamic_slice_in_dim(table, me * 32, 32, 2)
    there = lax.dynamic_slice_in_dim(table, (me ^ 1) * 32, 32, 2)
    weights = jnp.concatenate([here, there], axis=2).reshape(4, 4, 2, 64)
    loads = jnp.concatenate([mine, other], axis=0)
    return jnp.einsum("dfpn,nck->cdfpk", weights, loads, precision=HIGH)


def reduced(part, order, factor):
    me = lax.axis_index("freq")
    chip, core = me // 2, me % 2
    cut = HALF // 2

    def to(offset):
        return lax.dynamic_index_in_dim(part, (chip + offset) % 4, 1, False)

    far = to(2)
    from_left = ring(far[:cut], 1)
    from_right = ring(far[cut:], -1)
    right, left = to(1), to(3)
    right = jnp.concatenate([right[:cut] + from_left, right[cut:]], axis=0)
    left = jnp.concatenate([left[:cut], left[cut:] + from_right], axis=0)
    right, left, order = lax.optimization_barrier((right, left, order))
    ordered = reorder(order, factor)
    right, left, ordered = lax.optimization_barrier((ring(right, 1), ring(left, -1), ordered))
    total = to(0) + right + left
    total = total.reshape(GROUPS // 2, GC, 2, 2, 2, BS).transpose(2, 3, 0, 4, 1, 5)
    keep = lax.dynamic_index_in_dim(total, core, 0, False)
    got = swap(lax.dynamic_index_in_dim(total, 1 - core, 0, False))
    pair = jnp.where(core == 0, jnp.stack([keep, got], 1), jnp.stack([got, keep], 1))
    return pair.reshape(NB, 2, GC, BS), ordered


def split(value):
    high = value.astype(jnp.bfloat16)
    return high, (value - high.astype(jnp.float32)).astype(jnp.bfloat16)


def dot3(left, right, contract):
    dims = (((1,), (contract,)), ((), ()))

    def one(a, b):
        return lax.dot_general(a, b, dims, preferred_element_type=jnp.float32)

    return one(left[0], right[0]) + (one(left[0], right[1]) + one(left[1], right[0]))


def coupling_kernel(order_ref, inverse_ref, factor_ref, out_ref, below_ref, sem):
    me = lax.axis_index("rows")
    before = order_ref[0]
    for k in range(1, NB):
        before = jnp.where(order_ref[k] == me, order_ref[k - 1], before)
    at = pl.ds(pl.multiple_of(before * BS, BS), BS)
    copy = pltpu.make_async_copy(factor_ref.at[:, :, :, at], below_ref, sem)
    copy.start()
    copy.wait()
    for f in range(2):
        d_real, d_imag = split(inverse_ref[f, 0]), split(inverse_ref[f, 1])
        b_real, b_imag = split(below_ref[f, 0]), split(below_ref[f, 1])
        out_ref[f, 0] = dot3(d_real, b_real, 0) - dot3(d_imag, b_imag, 0)
        out_ref[f, 1] = dot3(d_real, b_imag, 0) + dot3(d_imag, b_real, 0)


def coupling_of(order, diag_inverse, factor):
    return pl.pallas_call(
        coupling_kernel,
        in_specs=[
            pl.BlockSpec(memory_space=pltpu.SMEM),
            pl.BlockSpec(memory_space=pltpu.VMEM),
            pl.BlockSpec(memory_space=pl.ANY),
        ],
        out_specs=pl.BlockSpec(memory_space=pltpu.VMEM),
        out_shape=jax.ShapeDtypeStruct((2, 2, BS, BS), jnp.float32),
        scratch_shapes=[pltpu.VMEM((2, 2, BS, BS), jnp.float32), pltpu.SemaphoreType.DMA],
        compiler_params=pltpu.CompilerParams(vmem_limit_bytes=WIDE),
        cost_estimate=pl.CostEstimate(flops=48 * BS**3, bytes_accessed=3 << 20, transcendentals=0),
        name="coupling",
    )(order, diag_inverse, factor)


def reorder_kernel(order_ref, factor_ref, *refs):
    outs, (held, in_sems, out_sems) = refs[: PAIRS + 1], refs[PAIRS + 1 :]
    reads, writes = [], []
    for k in range(NB - 1):
        at = pl.ds(pl.multiple_of(order_ref[k] * BS, BS), BS)
        reads.append(pltpu.make_async_copy(factor_ref.at[:, :, :, at], held.at[k], in_sems.at[k]))
        reads[k].start()
        side = (k + 1) % SPAN * BS if k else 0
        out = outs[(k + 1) // SPAN].at[:, :, :, side : side + BS]
        writes.append(pltpu.make_async_copy(held.at[k], out, out_sems.at[k]))
    for read, write in zip(reads, writes):
        read.wait()
        write.start()
    for write in writes:
        write.wait()


def reorder(order, factor):
    shapes = [jax.ShapeDtypeStruct((2, 2, BS, (SPAN if i else 1) * BS), jnp.float32) for i in range(PAIRS + 1)]
    return pl.pallas_call(
        reorder_kernel,
        in_specs=[pl.BlockSpec(memory_space=pltpu.SMEM), pl.BlockSpec(memory_space=pl.ANY)],
        out_specs=[pl.BlockSpec(memory_space=pl.ANY)] * (PAIRS + 1),
        out_shape=shapes,
        scratch_shapes=[
            pltpu.VMEM((NB - 1, 2, 2, BS, BS), jnp.float32),
            pltpu.SemaphoreType.DMA((NB - 1,)),
            pltpu.SemaphoreType.DMA((NB - 1,)),
        ],
        compiler_params=pltpu.CompilerParams(vmem_limit_bytes=WIDE),
        cost_estimate=pl.CostEstimate(flops=0, bytes_accessed=32 << 20, transcendentals=0),
        name="reorder",
    )(order, factor)


def links_kernel(order_ref, gathered_ref, *refs):
    outs, sems = refs[:PAIRS], refs[PAIRS]
    freq = lax.axis_index("rows") // GROUPS
    copies = []
    for pair in range(PAIRS):
        copies.append(
            pltpu.make_async_copy(gathered_ref.at[order_ref[SPAN * (pair + 1)], freq], outs[pair], sems.at[pair])
        )
        copies[-1].start()
    for copy in copies:
        copy.wait()


def links_of(order, gathered):
    return pl.pallas_call(
        links_kernel,
        in_specs=[pl.BlockSpec(memory_space=pltpu.SMEM), pl.BlockSpec(memory_space=pl.ANY)],
        out_specs=[pl.BlockSpec(memory_space=pl.ANY)] * PAIRS,
        out_shape=[jax.ShapeDtypeStruct((2, BS, BS), jnp.float32)] * PAIRS,
        scratch_shapes=[pltpu.SemaphoreType.DMA((PAIRS,))],
        compiler_params=pltpu.CompilerParams(vmem_limit_bytes=WIDE),
        cost_estimate=pl.CostEstimate(flops=0, bytes_accessed=8 << 20, transcendentals=0),
        name="links",
    )(order, gathered)


def local(kernel, shape, flops, name, *operands, scalars=0):
    specs = [pl.BlockSpec(memory_space=pltpu.SMEM)] * scalars
    specs += [pl.BlockSpec(memory_space=pltpu.VMEM)] * (len(operands) - scalars)
    return pl.pallas_call(
        kernel,
        in_specs=specs,
        out_specs=pl.BlockSpec(memory_space=pltpu.VMEM),
        out_shape=jax.ShapeDtypeStruct(shape, jnp.float32),
        compiler_params=pltpu.CompilerParams(vmem_limit_bytes=NARROW),
        cost_estimate=pl.CostEstimate(flops=flops, bytes_accessed=1 << 20, transcendentals=0),
        name=name,
    )(*operands)


def apply(matrix, vector):
    out = jnp.einsum("fpab,fgqcb->fgqcpa", matrix, vector, precision=HIGH)
    real = out[:, :, 0, :, 0] - out[:, :, 1, :, 1]
    imag = out[:, :, 1, :, 0] + out[:, :, 0, :, 1]
    return jnp.stack([real, imag], axis=2)


def solve_kernel(pair, order_ref, spread_ref, link_ref, out_ref):
    first = spread_ref[order_ref[SPAN * pair + 1]]
    second = spread_ref[order_ref[SPAN * pair + 2]]
    rows = split(first.reshape(2 * GC, BS))
    by_real, by_imag = [dot3(rows, split(link_ref[p]), 1).reshape(2, GC, BS) for p in range(2)]
    real = second[0] - (by_real[0] - by_imag[1])
    imag = second[1] - (by_real[1] + by_imag[0])
    out_ref[:, :, :BS] = first
    out_ref[0, :, BS:] = real
    out_ref[1, :, BS:] = imag


def solve(order, spread, link, pair):
    kernel = functools.partial(solve_kernel, pair)
    shape = (2, GC, SPAN * BS)
    return local(kernel, shape, 24 * BS * BS * GC, "solve", order, spread, link, scalars=1)


def exchange(value):
    return lax.all_to_all(value, "rows", 0, 0, tiled=True)


def body(time_loads, factor, diag_inverse, pivot_order):
    my_block = lax.axis_index("rows")
    my_place = jnp.sum(jnp.where(pivot_order == my_block, jnp.arange(NB, dtype=jnp.int32), 0))
    sent, order, time_loads = lax.optimization_barrier((half_of(time_loads, True), pivot_order, time_loads))
    other = swap(sent)
    coupling = coupling_of(order, diag_inverse, factor)
    gathered = lax.all_gather(coupling, "rows", axis=0)
    part = partial_spectra(half_of(time_loads, False), other)
    part, my_place = lax.optimization_barrier((part, my_place))
    residual, ordered = reduced(part, pivot_order, factor)
    residual = residual.reshape(2, GROUPS, 2, GC, BS)

    def spread():
        return exchange(apply(diag_inverse, residual).reshape(NB, 2, GC, BS))

    def updated(columns, block):
        return residual - apply(columns, block.reshape(2, GROUPS, 2, GC, -1))

    def share(block):
        return exchange(jnp.broadcast_to(block[None], (NB,) + block.shape))

    block = share(lax.dynamic_index_in_dim(spread(), pivot_order[0], 0, False))
    residual = updated(ordered[0], block)
    solved = [block]
    links = links_of(pivot_order, gathered)
    for pair in range(PAIRS):
        block = share(solve(pivot_order, spread(), links[pair], pair))
        solved.append(block)
        residual = updated(ordered[pair + 1], block)
    last = apply(diag_inverse, residual).reshape(NB, 2, GC, BS)

    def pick(place):
        at = (place + 1) % SPAN * BS if place else 0
        return lambda last, blocks: blocks[(place + 1) // SPAN][..., at : at + BS]

    own = lax.switch(my_place, [pick(i) for i in range(NB - 1)] + [lambda last, blocks: last], last, solved)
    own = own.reshape(2, GROUPS, 2, GC, BS).transpose(0, 2, 1, 3, 4)
    return own.reshape(2, 2, CASES, BS)


def solution(mesh):
    placed = (
        P("freq", None, "rows"),
        P("freq", None, "rows", None),
        P("freq", None, "rows", None),
        P(),
    )
    return jax.shard_map(
        body, mesh=mesh, in_specs=placed, out_specs=P("freq", None, None, "rows"), check_vma=False
    )
```
